32 devices in a mesh: owner: 16 (over z, y, x), section: 2 (over core).
Axes of the slice: x: 2, y: 2, z: 4, core: 2. Of those that a mesh axis runs over, the one named last changes fastest.
Arguments:
- memory: bfloat16 [65536, 512], P('owner', 'section'), may hold values from -6 to 6
- last_seen: int32 [65536], P('owner'), may hold values from 0 to 4095
- ends_owner: int32 [2, 1024, 2], P(None, 'owner'), may hold values from 0 to 15, all different within a row; in each aligned block of 64 rows (0 to 63, 64 to 127, ..., all dimensions but the last counted through in order) at most 16 rows name the same one
- ends_row: int32 [2, 1024, 2], P(None, 'owner'), may hold values from 0 to 4095
- event_order: int32 [2, 1024], P(None, 'owner'), may hold values from 0 to 1023, each once within a row
- event_time: int32 [2, 1024], P(None, 'owner'), may hold values from 0 to 4095
- edge_feat: bfloat16 [2, 1024, 128], P(None, 'owner'), may hold values from -6 to 6
- nb_owner: int32 [2, 1024, 40, 1], P(None, 'owner'), may hold values from 0 to 15; in each aligned block of 2560 rows (0 to 2559, 2560 to 5119, ..., all dimensions but the last counted through in order) at most 240 rows name the same one
- nb_row: int32 [2, 1024, 40], P(None, 'owner'), may hold values from 0 to 4095
- nb_time: int32 [2, 1024, 40], P(None, 'owner'), may hold values from 0 to 4095
- time_freq: float32 [128], replicated, may hold values from 0.001 to 1
- time_phase: float32 [128], replicated, may hold values from -3.140625 to 3.140625
- gru_in: bfloat16 [1280, 3, 512], P(None, None, 'section'), may hold values from -0.15625 to 0.15625
- gru_hid: bfloat16 [512, 3, 512], P(None, None, 'section'), may hold values from -0.25 to 0.25
- gru_bias: float32 [2, 3, 512], P(None, None, 'section'), may hold values from -3 to 3
- query_w: bfloat16 [512, 512], replicated, may hold values from -0.25 to 0.25
- key_w: bfloat16 [512, 512], replicated, may hold values from -0.25 to 0.25
- value_w: bfloat16 [512, 512], replicated, may hold values from -0.25 to 0.25
- time_key: bfloat16 [128, 512], replicated, may hold values from -0.5 to 0.5
- time_value: bfloat16 [128, 512], replicated, may hold values from -0.5 to 0.5
- out_w: bfloat16 [512, 512], replicated, may hold values from -0.25 to 0.25
Outputs:
- updated_memory: bfloat16 [65536, 512], P('owner', 'section')
- embedding: bfloat16 [2, 1024, 2, 512], P(None, 'owner', None, 'section')
The draws below stay inside these ranges and needn't reach their ends.
Inputs may be any that keep to these rules, and one draw needn't show every extreme that they name: `ends_owner`: in every batch the two endpoints of an event have different owners; of the events of one device (64 in a row in each batch), at most 16 name one owner, and in each draw some owner is named by exactly 16. `nb_owner`: in every batch, of the 2560 neighbor entries of one device's events, at most 240 name one owner, and in each draw some owner is named by exactly 240. `event_order`: each batch's row is a permutation of 0 to 1023; a larger value is a later event.
All inputs are finite; a program needn't handle non-finite values.
Results may differ from the reference program's by a relative error of at most 0.0029.
Values may be sent and summed in bfloat16 or wider, within the bound.
A program may use at most 128 MiB of HBM per device.

```python
import math
import jax
import jax.numpy as jnp
import numpy as np
from jax import lax

M = 512
TE = 128
EF = 128
HEADS = 2
NBR = 20
BATCHES = 2
EV_DEV = 64
ENT_ROWS = 4096
MSG = 1280
HD = 256
EVENTS = 1024
ENT = 65536
CAP = 16
CAPN = 240
N_OWNER = 16


def plant(values, key, low, largest):
    index_at = [jax.random.randint(jax.random.fold_in(key, axis), (), 0, length) for axis, length in enumerate(values.shape)]
    widest = values.shape.index(max(values.shape))
    beside = index_at[:widest] + [(index_at[widest] + 1) % values.shape[widest]] + index_at[widest + 1:]
    return values.at[tuple(index_at)].set(low).at[tuple(beside)].set(largest)


def levels(key, shape, split, smallest, high):
    def one(position, parts):
        draws = jax.random.uniform(jax.random.fold_in(jax.random.fold_in(key, 6), position), (parts,), jnp.float32, smallest / len(split), high / len(split))
        return jnp.repeat(jnp.exp(draws), shape[position] // parts).reshape((-1,) + (1,) * (len(shape) - position - 1))

    factor_of = one(*split[0])
    for cut in split[1:]:
        factor_of = factor_of * one(*cut)
    return factor_of


def rank_table(number_of, lean):
    loads = [(1 << 20) // math.isqrt(grade ** lean) + 1 for grade in range(1, number_of + 1)]
    spread = 1 + sum(loads) // (1 << 30)
    return np.cumsum(np.array([max(1, weight // spread) for weight in loads]))


def skewed_ids(key, shape, amount, skew):
    grid = rank_table(amount, skew)
    lot = jax.random.randint(jax.random.fold_in(key, 1), shape, 0, int(grid[amount - 1]))
    rank = jnp.searchsorted(jnp.asarray(grid, jnp.int32), lot, side="right")
    return jax.random.permutation(jax.random.fold_in(key, 2), amount)[rank].astype(jnp.int32)


def deal_out(own_key, own, number, rows, count, top, limit, lean):
    sequence = jax.random.permutation(own_key, count)
    packed, common = portions_of(count, rows * top, limit, lean, True), portions_of(count, rows * top, limit, lean, False)
    places = jnp.arange(count)

    def named(sizes, rotation):
        used = int((sizes > 0).sum())
        fixed = max(1, used // 4)
        moved = fixed + (places - fixed + rotation * (used - fixed)) % max(1, count - fixed)
        return jnp.zeros((count,), jnp.int32).at[sequence[jnp.where(places < fixed, places, moved)]].set(jnp.asarray(sizes, jnp.int32))

    sizes = jnp.where(number % 4 == 0, named(packed, number // 4), named(common, number - number // 4 - 1))
    mixed = jax.random.permutation(jax.random.fold_in(own, 3), count)
    source_of, taker = mixed[0:count // 2 * 2:2], mixed[1:count // 2 * 2:2]
    room = jnp.minimum(sizes[source_of] - 1, limit - sizes[taker]) // 2
    room = jnp.where((source_of == sequence[0]) | (taker == sequence[0]) | (sizes[taker] == 0), 0, jnp.maximum(room, 0))
    moved = jax.random.randint(jax.random.fold_in(own, 4), (count // 2,), 0, 1 << 20) % (room + 1)
    sizes = sizes.at[source_of].add(-moved).at[taker].add(moved)
    items = jnp.searchsorted(jnp.cumsum(sizes), jnp.arange(rows * top), side="right").astype(jnp.int32)
    table = items.reshape(top, rows).T
    table = table[jax.random.permutation(jax.random.fold_in(own, 1), rows)]
    rotation = jax.random.randint(jax.random.fold_in(own, 2), (rows, 1), 0, top)
    return jnp.take_along_axis(table, (jnp.arange(top)[None, :] + rotation) % top, axis=1)


def portions_of(amount, total, limit, lean, full):
    portions = [(1 << 20) // math.isqrt(standing ** lean) + 1 for standing in range(1, amount + 1)]
    largest = limit if full else min(limit, max(-(-total // amount), total * portions[0] // sum(portions)))
    least = 1 if total - largest >= amount - 1 else 0
    counts, spare = [largest] + [least] * (amount - 1), total - largest - least * (amount - 1)
    while spare > 0:
        candidates = [i for i in range(1, amount) if counts[i] < largest] or [i for i in range(1, amount) if counts[i] < limit]
        pool, budget = sum([portions[i] for i in candidates]), spare
        for i in candidates:
            addition = min(limit - counts[i], max(1, budget * portions[i] // pool), spare)
            counts[i] = counts[i] + addition
            spare = spare - addition
    return np.array(counts)


def gaussian(stream_key, shape, width, limit, split=(), kind=jnp.bfloat16):
    array = width * jax.random.normal(stream_key, shape, jnp.float32)
    if split:
        array = array * levels(stream_key, shape, split, -0.22, 0.18)
    return jnp.clip(array, -limit, limit).astype(kind)


def setup_inputs(seed: int = 0) -> dict:
    arg_keys = jax.random.split(jax.random.key(seed), 22)
    memory = gaussian(arg_keys[0], (ENT, M), 1.0, 6.0, ((0, 16), (1, 2)))
    last_seen = plant(jax.random.randint(arg_keys[1], (ENT,), 0, 4096), jax.random.fold_in(arg_keys[1], 1), 0, 4095).astype(jnp.int32)
    ends_owner_keys = jax.random.split(jax.random.fold_in(arg_keys[2], 1), BATCHES * EVENTS // EV_DEV)
    ends_owner_turns = jax.random.permutation(jax.random.fold_in(arg_keys[2], 3), BATCHES * EVENTS // EV_DEV)
    ends_owner = jax.vmap(lambda own, number: deal_out(jax.random.fold_in(arg_keys[2], 2), own, number, EV_DEV, N_OWNER, 2, CAP, 2))(ends_owner_keys, ends_owner_turns).reshape((BATCHES, EVENTS, 2))
    ends_row = plant(skewed_ids(arg_keys[3], (BATCHES, EVENTS, 2), ENT_ROWS, 2), jax.random.fold_in(arg_keys[3], 3), 0, ENT_ROWS - 1).astype(jnp.int32)
    event_order = jax.vmap(lambda own: jax.random.permutation(own, EVENTS))(jax.random.split(arg_keys[4], BATCHES)).reshape((BATCHES, EVENTS)).astype(jnp.int32)
    event_time = plant(jax.random.randint(arg_keys[5], (BATCHES, EVENTS), 0, 4096), jax.random.fold_in(arg_keys[5], 1), 0, 4095).astype(jnp.int32)
    edge_feat = gaussian(arg_keys[6], (BATCHES, EVENTS, EF), 1.0, 6.0, ((1, 16),))
    nb_owner_keys = jax.random.split(jax.random.fold_in(arg_keys[7], 1), BATCHES * EVENTS * (2 * NBR) // (2 * NBR * EV_DEV))
    nb_owner_turns = jax.random.permutation(jax.random.fold_in(arg_keys[7], 3), BATCHES * EVENTS * (2 * NBR) // (2 * NBR * EV_DEV))
    nb_owner = jax.vmap(lambda own, number: deal_out(jax.random.fold_in(arg_keys[7], 2), own, number, 2 * NBR * EV_DEV, N_OWNER, 1, CAPN, 2))(nb_owner_keys, nb_owner_turns).reshape((BATCHES, EVENTS, 2 * NBR, 1))
    nb_row = plant(skewed_ids(arg_keys[8], (BATCHES, EVENTS, 2 * NBR), ENT_ROWS, 2), jax.random.fold_in(arg_keys[8], 3), 0, ENT_ROWS - 1).astype(jnp.int32)
    nb_time = plant(jax.random.randint(arg_keys[9], (BATCHES, EVENTS, 2 * NBR), 0, 4096), jax.random.fold_in(arg_keys[9], 1), 0, 4095).astype(jnp.int32)
    time_freq = jnp.clip(jnp.exp(jax.random.uniform(arg_keys[10], (TE,), jnp.float32, math.log(0.001), math.log(1.0))), 0.001, 1.0)
    time_phase = jnp.clip(jax.random.uniform(arg_keys[11], (TE,), jnp.float32, -3.140625, 3.140625), -3.140625, 3.140625)
    gru_in = gaussian(arg_keys[12], (MSG, 3, M), MSG ** -0.5, 0.15625, ((2, 2),))
    gru_hid = gaussian(arg_keys[13], (M, 3, M), M ** -0.5, 0.25, ((2, 2),))
    gru_bias = gaussian(arg_keys[14], (2, 3, M), 0.5, 3.0, ((2, 2),), jnp.float32)
    query_w = gaussian(arg_keys[15], (M, M), M ** -0.5, 0.25)
    key_w = gaussian(arg_keys[16], (M, M), M ** -0.5, 0.25)
    value_w = gaussian(arg_keys[17], (M, M), M ** -0.5, 0.25)
    time_key = gaussian(arg_keys[18], (TE, M), TE ** -0.5, 0.5)
    time_value = gaussian(arg_keys[19], (TE, M), TE ** -0.5, 0.5)
    out_w = gaussian(arg_keys[20], (M, M), M ** -0.5, 0.25)
    return dict(memory=memory, last_seen=last_seen, ends_owner=ends_owner, ends_row=ends_row, event_order=event_order, event_time=event_time, edge_feat=edge_feat, nb_owner=nb_owner, nb_row=nb_row, nb_time=nb_time, time_freq=time_freq, time_phase=time_phase, gru_in=gru_in, gru_hid=gru_hid, gru_bias=gru_bias, query_w=query_w, key_w=key_w, value_w=value_w, time_key=time_key, time_value=time_value, out_w=out_w)


def time_code(delta, time_freq, time_phase):
    angle = delta.astype(jnp.float32)[..., None] * time_freq + time_phase
    return jnp.cos(angle).astype(jnp.bfloat16)

def reference(memory, last_seen, ends_owner, ends_row, event_order, event_time, edge_feat, nb_owner, nb_row, nb_time, time_freq, time_phase, gru_in, gru_hid, gru_bias, query_w, key_w, value_w, time_key, time_value, out_w):
    highest_level = lax.Precision.HIGHEST
    state = memory
    seen = last_seen
    per_head_keys = key_w.astype(jnp.float32).reshape(M, HEADS, HD)
    tkey_heads = time_key.astype(jnp.float32).reshape(TE, HEADS, HD)
    per_head_values = value_w.astype(jnp.float32).reshape(M, HEADS, HD)
    time_value_per_head = time_value.astype(jnp.float32).reshape(TE, HEADS, HD)
    out_full = out_w.astype(jnp.float32)
    results = []
    for batch in range(BATCHES):
        flat = (ends_owner[batch] * ENT_ROWS + ends_row[batch]).astype(jnp.int32).reshape(-1)
        ends = jnp.take(state, flat, axis=0)
        other = ends.reshape(EVENTS, 2, M)[:, ::-1].reshape(2 * EVENTS, M)
        time_two = jnp.repeat(event_time[batch], 2)
        self_code = time_code(time_two - jnp.take(seen, flat), time_freq, time_phase)
        feat_two = jnp.repeat(edge_feat[batch], 2, axis=0)
        message = jnp.concatenate([ends, other, self_code, feat_two], axis=1)
        from_msg = jnp.dot(message, gru_in.reshape(MSG, 3 * M), preferred_element_type=jnp.float32).reshape(-1, 3, M) + gru_bias[0]
        from_mem = jnp.dot(ends, gru_hid.reshape(M, 3 * M), preferred_element_type=jnp.float32).reshape(-1, 3, M) + gru_bias[1]
        reset = jax.nn.sigmoid(from_msg[:, 0] + from_mem[:, 0])
        update = jax.nn.sigmoid(from_msg[:, 1] + from_mem[:, 1])
        cand = jnp.tanh(from_msg[:, 2] + reset * from_mem[:, 2])
        fresh = ((1.0 - update) * cand + update * ends.astype(jnp.float32)).astype(jnp.bfloat16)
        near_ids = (nb_owner[batch][..., 0] * ENT_ROWS + nb_row[batch]).astype(jnp.int32).reshape(N_OWNER, 2 * EV_DEV, NBR)
        delta = (time_two.reshape(EVENTS, 2)[:, :, None] - nb_time[batch].reshape(EVENTS, 2, NBR)).reshape(N_OWNER, 2 * EV_DEV, NBR)
        own_rows = ends.reshape(N_OWNER, 2 * EV_DEV, M)

        def attend(block):
            ids, own, gap = block
            near = jnp.take(state, ids.reshape(-1), axis=0).reshape(ids.shape[0], NBR, M).astype(jnp.float32)
            code_near = time_code(gap, time_freq, time_phase).astype(jnp.float32)
            query_vector = jnp.dot(own, query_w, preferred_element_type=jnp.float32).reshape(-1, HEADS, HD)
            probe_vector = jnp.einsum('xuf,ouf->xuo', query_vector, per_head_keys, precision=highest_level)
            tprobe = jnp.einsum('phd,thd->pht', query_vector, tkey_heads, precision=highest_level)
            scores = (jnp.einsum('pjm,phm->pjh', near, probe_vector, precision=highest_level) + jnp.einsum('pjt,pht->pjh', code_near, tprobe, precision=highest_level)) / jnp.sqrt(jnp.float32(HD))
            weights = jnp.exp(scores)
            weights = weights / lax.optimization_barrier(jnp.sum(weights, axis=1, keepdims=True))
            pooled_result = jnp.einsum('pjh,pjm->phm', weights, near, precision=highest_level)
            pooled_encoding = jnp.einsum('pjh,pjt->pht', weights, code_near, precision=highest_level)
            attention_output = jnp.einsum('xzv,vzk->xzk', pooled_result, per_head_values, precision=highest_level) + jnp.einsum('ezo,ozy->ezy', pooled_encoding, time_value_per_head, precision=highest_level)
            emb = jnp.dot(attention_output.reshape(-1, M), out_full, precision=highest_level) + own.astype(jnp.float32)
            return emb.astype(jnp.bfloat16)
        emb = lax.map(attend, (near_ids, own_rows, delta))
        results.append(emb.reshape(EVENTS, 2, M))
        order_two = jnp.repeat(event_order[batch], 2)
        best = jnp.full((ENT,), -1, jnp.int32).at[flat].max(order_two)
        winner = order_two == jnp.take(best, flat)
        place = jnp.where(winner, flat, ENT).astype(jnp.int32)
        state = state.at[place].set(fresh, mode='drop')
        seen = seen.at[place].set(time_two, mode='drop')
    return (state, jnp.stack(results, axis=0))
```

```python
import functools
import math

import jax
import jax.numpy as jnp
from jax import lax
from jax.experimental import pallas as pl
from jax.experimental.pallas import tpu as pltpu
from jax.sharding import PartitionSpec as P

HEADS = 2
BATCHES = 2
BF = jnp.bfloat16
F32 = jnp.float32


def time_code(delta, time_freq, time_phase):
    angle = delta.astype(F32)[..., None] * time_freq + time_phase
    return jnp.cos(angle).astype(BF)


def owner_hits(own, owners):
    return own[..., None] == jnp.arange(owners, dtype=jnp.int32)


def ranks(hits, block):
    batches, total, owners = hits.shape
    parts = total // block
    cut = hits.astype(BF).reshape(batches, parts, block, owners)
    below = jnp.tril(jnp.ones((block, block), BF), -1)
    within = jnp.einsum("ij,bkjo->bkio", below, cut, preferred_element_type=F32)
    sums = jnp.sum(cut.astype(F32), axis=2)
    before = jnp.cumsum(sums, axis=1) - sums
    count = within + before[:, :, None]
    picked = jnp.sum(jnp.where(hits.reshape(cut.shape), count, 0.0), axis=3)
    return picked.reshape(batches, total).astype(jnp.int32)


def table_of(hits, rank, size, values):
    place = (rank[..., None] == jnp.arange(size, dtype=jnp.int32)).astype(BF)

    def digit(part):
        lhs = jnp.where(hits, part[..., None].astype(F32), 0.0).astype(BF)
        return jnp.einsum("bno,bns->bos", lhs, place, preferred_element_type=F32)

    return (digit(values // 64) * 64.0 + digit(values % 64)).astype(jnp.int32)


def attend_kernel(scale, group, near, code, query, wide, twide, out, num, den):
    step = pl.program_id(0)
    points, head = query.shape

    @pl.when(step == 0)
    def _():
        num[...] = jnp.zeros_like(num)
        den[...] = jnp.zeros_like(den)

    both = jnp.dot(near[...], wide[...], preferred_element_type=F32) + jnp.dot(
        code[...], twide[...], preferred_element_type=F32
    )
    q = query[...]
    for j in range(group):
        rows = both[j * points : (j + 1) * points]
        score = jnp.sum(rows[:, :head] * q, axis=1, keepdims=True) * scale
        weight = jnp.exp(score)
        den[...] += jnp.broadcast_to(weight, den.shape)
        num[...] += weight * rows[:, head:]

    @pl.when(step == pl.num_programs(0) - 1)
    def _():
        out[...] = num[...] / den[:, :1]


def attend(near, code, query, wide, twide, neighbors, scale):
    points, head = query.shape
    group = next(g for g in (4, 2, 1) if neighbors % g == 0)
    rows = group * points
    return pl.pallas_call(
        functools.partial(attend_kernel, scale, group),
        out_shape=jax.ShapeDtypeStruct((points, head), F32),
        grid=(neighbors // group,),
        in_specs=[
            pl.BlockSpec((rows, near.shape[1]), lambda i: (i, 0)),
            pl.BlockSpec((rows, code.shape[1]), lambda i: (i, 0)),
            pl.BlockSpec(query.shape, lambda i: (0, 0)),
            pl.BlockSpec(wide.shape, lambda i: (0, 0)),
            pl.BlockSpec(twide.shape, lambda i: (0, 0)),
        ],
        out_specs=pl.BlockSpec((points, head), lambda i: (0, 0)),
        scratch_shapes=[pltpu.VMEM((points, head), F32), pltpu.VMEM((points, 128), F32)],
        compiler_params=pltpu.CompilerParams(vmem_limit_bytes=24 * 1024 * 1024),
        cost_estimate=pl.CostEstimate(
            flops=2 * near.shape[0] * (near.shape[1] + code.shape[1]) * wide.shape[1],
            bytes_accessed=2 * near.size + 2 * code.size + 2 * wide.size,
            transcendentals=near.shape[0],
        ),
    )(near, code, query, wide, twide)


def write_rows(memory, rows, order, values):
    count = memory.shape[0]
    beaten = jnp.any((rows[:, None] == rows[None, :]) & (order[None, :] > order[:, None]), axis=1)
    place = jnp.where((rows >= 0) & ~beaten, rows, count)
    return memory.at[place].set(values, mode="drop")


def on_device(
    memory,
    last_seen,
    ends_owner,
    ends_row,
    event_order,
    event_time,
    edge_feat,
    nb_owner,
    nb_row,
    nb_time,
    time_freq,
    time_phase,
    gru_in,
    gru_hid,
    gru_bias,
    query_w,
    key_w,
    value_w,
    time_key,
    time_value,
    out_w,
):
    owners = lax.axis_size("owner")
    sections = lax.axis_size("section")
    count, half = memory.shape
    width = half * sections
    events = ends_owner.shape[1]
    points = 2 * events
    neighbors = nb_row.shape[2] // 2
    head_dim = width // HEADS
    cap = max(4, 4 * events // owners)
    capn = max(8, 3 * neighbors * events // owners)
    slots = cap + capn
    total = owners * points
    scale = 1.0 / math.sqrt(head_dim)
    section_pos = lax.axis_index("section")
    owner_pos = lax.axis_index("owner")

    def by_neighbor(x):
        return x.reshape(BATCHES, points, neighbors).swapaxes(1, 2)

    end_own = ends_owner.reshape(BATCHES, points)
    end_row = ends_row.reshape(BATCHES, points)
    near_own = by_neighbor(nb_owner[..., 0]).reshape(BATCHES, -1)
    near_row = by_neighbor(nb_row).reshape(BATCHES, -1)
    order_two = jnp.repeat(event_order, 2, axis=1)
    time_two = jnp.repeat(event_time, 2, axis=1)
    end_hits = owner_hits(end_own, owners)
    near_hits = owner_hits(near_own, owners)
    end_rank = ranks(end_hits, points)
    near_rank = ranks(near_hits, points)
    local = jnp.broadcast_to(jnp.arange(points, dtype=jnp.int32), (BATCHES, points))
    asked = jnp.concatenate(
        [
            table_of(end_hits, end_rank, cap, end_row + 1),
            table_of(near_hits, near_rank, capn, near_row + 1),
            table_of(end_hits, end_rank, cap, order_two),
            table_of(end_hits, end_rank, cap, local),
        ],
        axis=2,
    )
    got = lax.all_to_all(asked.swapaxes(0, 1), "owner", split_axis=0, concat_axis=0, tiled=True)
    end_slot = end_own * slots + end_rank
    near_slot = near_own * slots + cap + near_rank

    end_id = end_own * count + end_row
    near_id = near_own * count + near_row
    mine = owner_pos * points + jnp.arange(points, dtype=jnp.int32)
    meta = jnp.stack([end_id[0], order_two[0] * total + mine, time_two[0]])
    all_meta = lax.all_gather(meta, "owner", axis=1, tiled=True)
    all_seen = lax.all_gather(last_seen, "owner", axis=0, tiled=True)
    base_seen = jnp.take(all_seen, end_id, mode="clip")

    came = []
    for batch in range(BATCHES):
        rows = jnp.maximum(got[:, batch, :slots] - 1, 0).reshape(-1)
        looked = jnp.take(memory, rows, axis=0, mode="clip").reshape(owners, slots, half)
        came.append(
            lax.all_to_all(looked, "owner", split_axis=0, concat_axis=0, tiled=True).reshape(-1, half)
        )

    start = section_pos * head_dim

    def columns(w, at, size):
        return lax.dynamic_slice_in_dim(w, at, size, 1)

    wide = jnp.concatenate([columns(key_w, start, head_dim), columns(value_w, start, head_dim)], axis=1)
    twide = jnp.concatenate(
        [columns(time_key, start, head_dim), columns(time_value, start, head_dim)], axis=1
    )
    query_cols = columns(query_w, start, head_dim)
    own_cols = columns(out_w, section_pos * half, half).astype(F32)
    gru_in_flat = gru_in.reshape(gru_in.shape[0], 3 * half)
    gru_hid_flat = gru_hid.reshape(width, 3 * half)
    near_code = time_code(time_two[:, None] - by_neighbor(nb_time), time_freq, time_phase)
    near_code = near_code.reshape(BATCHES, neighbors * points, -1)

    results = []
    updated = memory
    fresh_all = None
    for batch in range(BATCHES):
        table = came[batch]
        pick_end = end_slot[batch]
        pick_near = near_slot[batch]
        seen = base_seen[batch]
        if batch > 0:
            ids = jnp.concatenate([end_id[batch], near_id[batch]])
            best = jnp.max(
                jnp.where(all_meta[0][:, None] == ids[None, :], all_meta[1][:, None], -1), axis=0
            )
            written = best >= 0
            index = jnp.where(written, best % total, 0)
            table = jnp.concatenate([table, fresh_all], axis=0)
            newer = owners * slots + index
            pick_end = jnp.where(written[:points], newer[:points], pick_end)
            pick_near = jnp.where(written[points:], newer[points:], pick_near)
            since = jnp.take(all_meta[2], index[:points], mode="clip")
            seen = jnp.where(written[:points], since, seen)
        pick_other = pick_end.reshape(events, 2)[:, ::-1].reshape(points)
        picked = jnp.take(
            table, jnp.concatenate([pick_end, pick_other, pick_near]), axis=0, mode="clip"
        )
        full = lax.all_gather(picked, "section", axis=1, tiled=True)
        end_half = picked[:points].astype(F32)
        end_full = full[:points]
        other = full[points : 2 * points]
        near_full = full[2 * points :]
        self_code = time_code(time_two[batch] - seen, time_freq, time_phase)
        feat_two = jnp.repeat(edge_feat[batch], 2, axis=0)
        message = jnp.concatenate([end_full, other, self_code, feat_two], axis=1)
        from_msg = jnp.dot(message, gru_in_flat, preferred_element_type=F32)
        from_mem = jnp.dot(end_full, gru_hid_flat, preferred_element_type=F32)

        def block(x, i, side):
            return x[:, i * half : (i + 1) * half] + gru_bias[side, i]

        reset = jax.nn.sigmoid(block(from_msg, 0, 0) + block(from_mem, 0, 1))
        update = jax.nn.sigmoid(block(from_msg, 1, 0) + block(from_mem, 1, 1))
        cand = jnp.tanh(block(from_msg, 2, 0) + reset * block(from_mem, 2, 1))
        fresh = ((1.0 - update) * cand + update * end_half).astype(BF)
        fresh_all = lax.all_gather(fresh, "owner", axis=0, tiled=True)

        wrote = got[:, batch, :cap].reshape(-1) - 1
        order = got[:, batch, slots : slots + cap].reshape(-1)
        source = jnp.arange(owners, dtype=jnp.int32)[:, None] * points + got[:, batch, slots + cap :]
        values = jnp.take(fresh_all, source.reshape(-1), axis=0, mode="clip")
        updated = write_rows(updated, wrote, order, values)

        query = jnp.dot(end_full, query_cols, preferred_element_type=F32)
        attended = attend(near_full, near_code[batch], query, wide, twide, neighbors, scale)
        mixed = lax.all_gather(attended, "section", axis=1, tiled=True)
        emb = jnp.dot(mixed, own_cols, precision=lax.Precision.HIGHEST) + end_half
        results.append(emb.astype(BF).reshape(events, 2, half))
    return (updated, jnp.stack(results, axis=0))


def solution(mesh):
    in_specs = (
        P("owner", "section"),
        P("owner"),
        P(None, "owner", None),
        P(None, "owner", None),
        P(None, "owner"),
        P(None, "owner"),
        P(None, "owner", None),
        P(None, "owner", None, None),
        P(None, "owner", None),
        P(None, "owner", None),
        P(),
        P(),
        P(None, None, "section"),
        P(None, None, "section"),
        P(None, None, "section"),
        P(),
        P(),
        P(),
        P(),
        P(),
        P(),
    )
    out_specs = (P("owner", "section"), P(None, "owner", None, "section"))
    return jax.shard_map(
        on_device, mesh=mesh, in_specs=in_specs, out_specs=out_specs, check_vma=False
    )
```

```python
import functools
import math

import jax
import jax.numpy as jnp
from jax import lax
from jax.experimental import pallas as pl
from jax.experimental.pallas import tpu as pltpu
from jax.sharding import PartitionSpec as P

HEADS = 2
BATCHES = 2
BF = jnp.bfloat16
F32 = jnp.float32


def time_code(delta, time_freq, time_phase):
    angle = delta.astype(F32)[..., None] * time_freq + time_phase
    return jnp.cos(angle).astype(BF)


def owner_hits(own, owners):
    return own[..., None] == jnp.arange(owners, dtype=jnp.int32)


def ranks(hits, block):
    batches, total, owners = hits.shape
    parts = total // block
    cut = hits.astype(BF).reshape(batches, parts, block, owners)
    below = jnp.tril(jnp.ones((block, block), BF), -1)
    within = jnp.einsum("ij,bkjo->bkio", below, cut, preferred_element_type=F32)
    sums = jnp.sum(cut.astype(F32), axis=2).astype(BF)
    earlier = jnp.tril(jnp.ones((parts, parts), BF), -1)
    before = jnp.einsum("kl,blo->bko", earlier, sums, preferred_element_type=F32)
    count = within + before[:, :, None]
    picked = jnp.sum(jnp.where(hits.reshape(cut.shape), count, 0.0), axis=3)
    return picked.reshape(batches, total).astype(jnp.int32)


def table_of(hits, rank, size, values):
    place = (rank[..., None] == jnp.arange(size, dtype=jnp.int32)).astype(BF)

    def digit(part):
        lhs = jnp.where(hits, part[..., None].astype(F32), 0.0).astype(BF)
        return jnp.einsum("bno,bns->bos", lhs, place, preferred_element_type=F32)

    return (digit(values // 64) * 64.0 + digit(values % 64)).astype(jnp.int32)


def attend_kernel(scale, group, near, code, query, wide, twide, out, num, den):
    step = pl.program_id(0)
    points, head = query.shape

    @pl.when(step == 0)
    def _():
        num[...] = jnp.zeros_like(num)
        den[...] = jnp.zeros_like(den)

    both = jnp.dot(near[...], wide[...], preferred_element_type=F32) + jnp.dot(
        code[...], twide[...], preferred_element_type=F32
    )
    q = query[...]
    for j in range(group):
        rows = both[j * points : (j + 1) * points]
        score = jnp.sum(rows[:, :head] * q, axis=1, keepdims=True) * scale
        weight = jnp.exp(score)
        den[...] += jnp.broadcast_to(weight, den.shape)
        num[...] += weight * rows[:, head:]

    @pl.when(step == pl.num_programs(0) - 1)
    def _():
        out[...] = num[...] / den[:, :1]


def attend(near, code, query, wide, twide, neighbors, scale):
    points, head = query.shape
    group = next(g for g in (4, 2, 1) if neighbors % g == 0)
    rows = group * points
    return pl.pallas_call(
        functools.partial(attend_kernel, scale, group),
        out_shape=jax.ShapeDtypeStruct((points, head), F32),
        grid=(neighbors // group,),
        in_specs=[
            pl.BlockSpec((rows, near.shape[1]), lambda i: (i, 0)),
            pl.BlockSpec((rows, code.shape[1]), lambda i: (i, 0)),
            pl.BlockSpec(query.shape, lambda i: (0, 0)),
            pl.BlockSpec(wide.shape, lambda i: (0, 0)),
            pl.BlockSpec(twide.shape, lambda i: (0, 0)),
        ],
        out_specs=pl.BlockSpec((points, head), lambda i: (0, 0)),
        scratch_shapes=[pltpu.VMEM((points, head), F32), pltpu.VMEM((points, 128), F32)],
        compiler_params=pltpu.CompilerParams(vmem_limit_bytes=24 * 1024 * 1024),
        cost_estimate=pl.CostEstimate(
            flops=2 * code.shape[0] * (near.shape[1] + code.shape[1]) * wide.shape[1],
            bytes_accessed=2 * code.shape[0] * near.shape[1] + 2 * code.size + 2 * wide.size,
            transcendentals=code.shape[0],
        ),
    )(near, code, query, wide, twide)


def exchange(x):
    return lax.all_to_all(x, "owner", split_axis=0, concat_axis=0, tiled=True)


def write_rows(memory, rows, order, values):
    count = memory.shape[0]
    beaten = jnp.any((rows[:, None] == rows[None, :]) & (order[None, :] > order[:, None]), axis=1)
    place = jnp.where((rows >= 0) & ~beaten, rows, count)
    return memory.at[place].set(values, mode="drop")


def on_device(
    memory,
    last_seen,
    ends_owner,
    ends_row,
    event_order,
    event_time,
    edge_feat,
    nb_owner,
    nb_row,
    nb_time,
    time_freq,
    time_phase,
    gru_in,
    gru_hid,
    gru_bias,
    query_w,
    key_w,
    value_w,
    time_key,
    time_value,
    out_w,
):
    owners = lax.axis_size("owner")
    sections = lax.axis_size("section")
    count, half = memory.shape
    width = half * sections
    events = ends_owner.shape[1]
    points = 2 * events
    neighbors = nb_row.shape[2] // 2
    head_dim = width // HEADS
    cap = max(4, 4 * events // owners)
    capn = max(8, 3 * neighbors * events // owners)
    slots = cap + capn
    total = owners * points
    scale = 1.0 / math.sqrt(head_dim)
    section_pos = lax.axis_index("section")
    owner_pos = lax.axis_index("owner")

    def by_neighbor(x):
        return x.reshape(BATCHES, points, neighbors).swapaxes(1, 2)

    end_own = ends_owner.reshape(BATCHES, points)
    end_row = ends_row.reshape(BATCHES, points)
    near_own = by_neighbor(nb_owner[..., 0]).reshape(BATCHES, -1)
    near_row = by_neighbor(nb_row).reshape(BATCHES, -1)
    order_two = jnp.repeat(event_order, 2, axis=1)
    time_two = jnp.repeat(event_time, 2, axis=1)
    end_hits = owner_hits(end_own, owners)
    near_hits = owner_hits(near_own, owners)
    end_rank = ranks(end_hits, points)
    near_rank = ranks(near_hits, points)
    local = jnp.broadcast_to(jnp.arange(points, dtype=jnp.int32), (BATCHES, points))
    asked = jnp.concatenate(
        [
            table_of(end_hits, end_rank, cap, end_row + 1),
            table_of(near_hits, near_rank, capn, near_row + 1),
            table_of(end_hits, end_rank, cap, order_two),
            table_of(end_hits, end_rank, cap, local),
        ],
        axis=2,
    )
    end_id = end_own * count + end_row
    near_id = near_own * count + near_row
    mine = owner_pos * points + jnp.arange(points, dtype=jnp.int32)
    meta = jnp.concatenate([end_id[0], order_two[0] * total + mine, time_two[0]])
    per_batch = slots + 2 * cap
    asked = jnp.concatenate(
        [
            asked.swapaxes(0, 1).reshape(owners, BATCHES * per_batch),
            jnp.broadcast_to(meta, (owners, 3 * points)),
        ],
        axis=1,
    )
    answer = exchange(asked)
    got = answer[:, : BATCHES * per_batch].reshape(owners, BATCHES, per_batch)
    all_meta = answer[:, BATCHES * per_batch :].reshape(owners, 3, points)
    all_meta = [all_meta[:, i].reshape(total) for i in range(3)]
    end_pos = end_own * cap + end_rank
    end_slot = end_own * slots + end_rank
    near_slot = near_own * slots + cap + near_rank

    asked_ends = jnp.maximum(got[:, :, :cap] - 1, 0).reshape(-1)
    stamps = jnp.take(last_seen, asked_ends, mode="clip").reshape(owners, BATCHES * cap)
    stamps = exchange(stamps).reshape(owners, BATCHES, cap).swapaxes(0, 1).reshape(BATCHES, -1)
    base_seen = jnp.stack([jnp.take(stamps[b], end_pos[b], mode="clip") for b in range(BATCHES)])

    def look(batch):
        rows = jnp.maximum(got[:, batch, :slots] - 1, 0).reshape(-1)
        return jnp.take(memory, rows, axis=0, mode="clip").reshape(owners, slots, half)

    start = section_pos * head_dim

    def columns(w, at, size):
        return lax.dynamic_slice_in_dim(w, at, size, 1)

    wide = jnp.concatenate([columns(key_w, start, head_dim), columns(value_w, start, head_dim)], axis=1)
    twide = jnp.concatenate(
        [columns(time_key, start, head_dim), columns(time_value, start, head_dim)], axis=1
    )
    query_cols = columns(query_w, start, head_dim)
    own_cols = columns(out_w, section_pos * half, half).astype(F32)
    gru_in_flat = gru_in.reshape(gru_in.shape[0], 3 * half)
    gru_hid_flat = gru_hid.reshape(width, 3 * half)
    near_code = time_code(time_two[:, None] - by_neighbor(nb_time), time_freq, time_phase)
    near_code = near_code.reshape(BATCHES, neighbors * points, -1)

    first, second = exchange(look(0)), look(1)
    first, second, near_code, gru_in_flat, gru_hid_flat = lax.optimization_barrier(
        (first, second, near_code, gru_in_flat, gru_hid_flat)
    )
    came = [first.reshape(-1, half), exchange(second).reshape(-1, half)]

    results = []
    updated = memory
    fresh_all = None
    for batch in range(BATCHES):
        table = came[batch]
        pick_end = end_slot[batch]
        pick_near = near_slot[batch]
        seen = base_seen[batch]
        if batch > 0:
            ids = jnp.concatenate([end_id[batch], near_id[batch]])
            best = jnp.max(
                jnp.where(all_meta[0][:, None] == ids[None, :], all_meta[1][:, None], -1), axis=0
            )
            written = best >= 0
            index = jnp.where(written, best % total, 0)
            table, results[0] = lax.optimization_barrier((table, results[0]))
            table = jnp.concatenate([table, fresh_all], axis=0)
            newer = owners * slots + index
            pick_end = jnp.where(written[:points], newer[:points], pick_end)
            pick_near = jnp.where(written[points:], newer[points:], pick_near)
            since = jnp.take(all_meta[2], index[:points], mode="clip")
            seen = jnp.where(written[:points], since, seen)
        pick_other = pick_end.reshape(events, 2)[:, ::-1].reshape(points)
        picked = jnp.take(
            table, jnp.concatenate([pick_near, pick_end, pick_other]), axis=0, mode="clip"
        )
        full = lax.all_gather(picked, "section", axis=1, tiled=True)
        near_count = neighbors * points
        end_half = picked[near_count : near_count + points].astype(F32)
        end_full = full[near_count : near_count + points]
        other = full[near_count + points :]
        self_code = time_code(time_two[batch] - seen, time_freq, time_phase)
        feat_two = jnp.repeat(edge_feat[batch], 2, axis=0)
        message = jnp.concatenate([end_full, other, self_code, feat_two], axis=1)
        from_msg = jnp.dot(message, gru_in_flat, preferred_element_type=F32)
        from_mem = jnp.dot(end_full, gru_hid_flat, preferred_element_type=F32)

        def block(x, i, side):
            return x[:, i * half : (i + 1) * half] + gru_bias[side, i]

        reset = jax.nn.sigmoid(block(from_msg, 0, 0) + block(from_mem, 0, 1))
        update = jax.nn.sigmoid(block(from_msg, 1, 0) + block(from_mem, 1, 1))
        cand = jnp.tanh(block(from_msg, 2, 0) + reset * block(from_mem, 2, 1))
        fresh = ((1.0 - update) * cand + update * end_half).astype(BF)
        wrote = got[:, batch, :cap].reshape(-1) - 1
        order = got[:, batch, slots : slots + cap].reshape(-1)
        if batch + 1 < BATCHES:
            fresh_all = exchange(jnp.broadcast_to(fresh, (owners, points, half))).reshape(total, half)
            source = jnp.arange(owners, dtype=jnp.int32)[:, None] * points
            source = source + got[:, batch, slots + cap :]
            values = jnp.take(fresh_all, source.reshape(-1), axis=0, mode="clip")
        else:
            place = jnp.arange(owners * cap, dtype=jnp.int32)[:, None] == end_pos[batch][None, :]
            sent = jnp.dot(place.astype(BF), fresh, preferred_element_type=F32).astype(BF)
            values = exchange(sent.reshape(owners, cap, half)).reshape(-1, half)
        updated = write_rows(updated, wrote, order, values)

        query = jnp.dot(end_full, query_cols, preferred_element_type=F32)
        attended = attend(full, near_code[batch], query, wide, twide, neighbors, scale)
        mixed = lax.all_gather(attended, "section", axis=1, tiled=True)
        emb = jnp.dot(mixed, own_cols, precision=lax.Precision.HIGHEST) + end_half
        results.append(emb.astype(BF).reshape(events, 2, half))
    return (updated, jnp.stack(results, axis=0))


def solution(mesh):
    in_specs = (
        P("owner", "section"),
        P("owner"),
        P(None, "owner", None),
        P(None, "owner", None),
        P(None, "owner"),
        P(None, "owner"),
        P(None, "owner", None),
        P(None, "owner", None, None),
        P(None, "owner", None),
        P(None, "owner", None),
        P(),
        P(),
        P(None, None, "section"),
        P(None, None, "section"),
        P(None, None, "section"),
        P(),
        P(),
        P(),
        P(),
        P(),
        P(),
    )
    out_specs = (P("owner", "section"), P(None, "owner", None, "section"))
    return jax.shard_map(
        on_device, mesh=mesh, in_specs=in_specs, out_specs=out_specs, check_vma=False
    )
```

```python
import functools
import math

import jax
import jax.numpy as jnp
from jax import lax
from jax.experimental import pallas as pl
from jax.experimental.pallas import tpu as pltpu
from jax.sharding import PartitionSpec as P

HEADS = 2
BATCHES = 2
BF = jnp.bfloat16
F32 = jnp.float32


def time_code(delta, time_freq, time_phase):
    angle = delta.astype(F32)[..., None] * time_freq + time_phase
    return jnp.cos(angle).astype(BF)


def owner_hits(own, owners):
    return own[..., None] == jnp.arange(owners, dtype=jnp.int32)


def ranks(hits, block):
    batches, total, owners = hits.shape
    parts = total // block
    cut = hits.astype(BF).reshape(batches, parts, block, owners)
    below = jnp.tril(jnp.ones((block, block), BF), -1)
    within = jnp.einsum("ij,bkjo->bkio", below, cut, preferred_element_type=F32)
    sums = jnp.sum(cut.astype(F32), axis=2).astype(BF)
    earlier = jnp.tril(jnp.ones((parts, parts), BF), -1)
    before = jnp.einsum("kl,blo->bko", earlier, sums, preferred_element_type=F32)
    count = within + before[:, :, None]
    picked = jnp.sum(jnp.where(hits.reshape(cut.shape), count, 0.0), axis=3)
    return picked.reshape(batches, total).astype(jnp.int32)


def table_of(hits, rank, size, values):
    place = (rank[..., None] == jnp.arange(size, dtype=jnp.int32)).astype(BF)

    def digit(part):
        lhs = jnp.where(hits, part[..., None].astype(F32), 0.0).astype(BF)
        return jnp.einsum("bno,bns->bos", lhs, place, preferred_element_type=F32)

    return (digit(values // 64) * 64.0 + digit(values % 64)).astype(jnp.int32)


def attend_kernel(scale, group, near, code, query, wide, twide, out, num, den):
    step = pl.program_id(0)
    points, head = query.shape

    @pl.when(step == 0)
    def _():
        num[...] = jnp.zeros_like(num)
        den[...] = jnp.zeros_like(den)

    both = jnp.dot(near[...], wide[...], preferred_element_type=F32) + jnp.dot(
        code[...], twide[...], preferred_element_type=F32
    )
    q = query[...]
    for j in range(group):
        rows = both[j * points : (j + 1) * points]
        score = jnp.sum(rows[:, :head] * q, axis=1, keepdims=True) * scale
        weight = jnp.exp(score)
        den[...] += jnp.broadcast_to(weight, den.shape)
        num[...] += weight * rows[:, head:]

    @pl.when(step == pl.num_programs(0) - 1)
    def _():
        out[...] = num[...] / den[:, :1]


def attend(near, code, query, wide, twide, neighbors, scale):
    points, head = query.shape
    group = next(g for g in (4, 2, 1) if neighbors % g == 0)
    rows = group * points
    return pl.pallas_call(
        functools.partial(attend_kernel, scale, group),
        out_shape=jax.ShapeDtypeStruct((points, head), F32),
        grid=(neighbors // group,),
        in_specs=[
            pl.BlockSpec((rows, near.shape[1]), lambda i: (i, 0)),
            pl.BlockSpec((rows, code.shape[1]), lambda i: (i, 0)),
            pl.BlockSpec(query.shape, lambda i: (0, 0)),
            pl.BlockSpec(wide.shape, lambda i: (0, 0)),
            pl.BlockSpec(twide.shape, lambda i: (0, 0)),
        ],
        out_specs=pl.BlockSpec((points, head), lambda i: (0, 0)),
        scratch_shapes=[pltpu.VMEM((points, head), F32), pltpu.VMEM((points, 128), F32)],
        compiler_params=pltpu.CompilerParams(vmem_limit_bytes=24 * 1024 * 1024),
        cost_estimate=pl.CostEstimate(
            flops=2 * code.shape[0] * (near.shape[1] + code.shape[1]) * wide.shape[1],
            bytes_accessed=2 * code.shape[0] * near.shape[1] + 2 * code.size + 2 * wide.size,
            transcendentals=code.shape[0],
        ),
    )(near, code, query, wide, twide)


def exchange(x):
    return lax.all_to_all(x, "owner", split_axis=0, concat_axis=0, tiled=True)


def gather_by_doubling(x, owners):
    bit = owners // 2
    while bit:
        pairs = [(i, i ^ bit) for i in range(owners)]
        x = jnp.concatenate([x, lax.ppermute(x, "owner", pairs)], axis=0)
        bit //= 2
    return x


def place_by_doubling(owner, this, owners):
    differ, place, bit, unit = owner ^ this, jnp.zeros_like(owner), owners // 2, 1
    while bit:
        place = place + jnp.where((differ & bit) != 0, unit, 0)
        bit, unit = bit // 2, unit * 2
    return place


def write_rows(memory, rows, order, values):
    count = memory.shape[0]
    beaten = jnp.any((rows[:, None] == rows[None, :]) & (order[None, :] > order[:, None]), axis=1)
    place = jnp.where((rows >= 0) & ~beaten, rows, count)
    return memory.at[place].set(values, mode="drop")


def on_device(
    memory,
    last_seen,
    ends_owner,
    ends_row,
    event_order,
    event_time,
    edge_feat,
    nb_owner,
    nb_row,
    nb_time,
    time_freq,
    time_phase,
    gru_in,
    gru_hid,
    gru_bias,
    query_w,
    key_w,
    value_w,
    time_key,
    time_value,
    out_w,
):
    owners = lax.axis_size("owner")
    sections = lax.axis_size("section")
    count, half = memory.shape
    width = half * sections
    events = ends_owner.shape[1]
    points = 2 * events
    neighbors = nb_row.shape[2] // 2
    head_dim = width // HEADS
    cap = max(4, 4 * events // owners)
    capn = max(8, 3 * neighbors * events // owners)
    slots = cap + capn
    total = owners * points
    scale = 1.0 / math.sqrt(head_dim)
    section_pos = lax.axis_index("section")
    owner_pos = lax.axis_index("owner")

    def by_neighbor(x):
        return x.reshape(BATCHES, points, neighbors).swapaxes(1, 2)

    end_own = ends_owner.reshape(BATCHES, points)
    end_row = ends_row.reshape(BATCHES, points)
    near_own = by_neighbor(nb_owner[..., 0]).reshape(BATCHES, -1)
    near_row = by_neighbor(nb_row).reshape(BATCHES, -1)
    order_two = jnp.repeat(event_order, 2, axis=1)
    time_two = jnp.repeat(event_time, 2, axis=1)
    end_hits = owner_hits(end_own, owners)
    near_hits = owner_hits(near_own, owners)
    end_rank = ranks(end_hits, points)
    near_rank = ranks(near_hits, points)
    local = jnp.broadcast_to(jnp.arange(points, dtype=jnp.int32), (BATCHES, points))
    asked = jnp.concatenate(
        [
            table_of(end_hits, end_rank, cap, end_row + 1),
            table_of(near_hits, near_rank, capn, near_row + 1),
            table_of(end_hits, end_rank, cap, order_two),
            table_of(end_hits, end_rank, cap, local),
        ],
        axis=2,
    )
    end_id = end_own * count + end_row
    near_id = near_own * count + near_row
    mine = owner_pos * points + jnp.arange(points, dtype=jnp.int32)
    meta = jnp.concatenate([end_id[0], order_two[0] * total + mine, time_two[0]])
    per_batch = slots + 2 * cap
    asked = jnp.concatenate(
        [
            asked.swapaxes(0, 1).reshape(owners, BATCHES * per_batch),
            jnp.broadcast_to(meta, (owners, 3 * points)),
        ],
        axis=1,
    )
    answer = exchange(asked)
    got = answer[:, : BATCHES * per_batch].reshape(owners, BATCHES, per_batch)
    all_meta = answer[:, BATCHES * per_batch :].reshape(owners, 3, points)
    all_meta = [all_meta[:, i].reshape(total) for i in range(3)]
    end_pos = end_own * cap + end_rank
    end_slot = end_own * slots + end_rank
    near_slot = near_own * slots + cap + near_rank

    asked_ends = jnp.maximum(got[:, :, :cap] - 1, 0).reshape(-1)
    stamps = jnp.take(last_seen, asked_ends, mode="clip").reshape(owners, BATCHES * cap)
    stamps = exchange(stamps)

    def look(batch):
        rows = jnp.maximum(got[:, batch, :slots] - 1, 0).reshape(-1)
        return jnp.take(memory, rows, axis=0, mode="clip").reshape(owners, slots, half)

    start = section_pos * head_dim

    def columns(w, at, size):
        return lax.dynamic_slice_in_dim(w, at, size, 1)

    wide = jnp.concatenate([columns(key_w, start, head_dim), columns(value_w, start, head_dim)], axis=1)
    twide = jnp.concatenate(
        [columns(time_key, start, head_dim), columns(time_value, start, head_dim)], axis=1
    )
    query_cols = columns(query_w, start, head_dim)
    own_cols = columns(out_w, section_pos * half, half).astype(F32)
    gru_in_flat = gru_in.reshape(gru_in.shape[0], 3 * half)
    gru_hid_flat = gru_hid.reshape(width, 3 * half)
    near_code = time_code(time_two[:, None] - by_neighbor(nb_time), time_freq, time_phase)
    near_code = near_code.reshape(BATCHES, neighbors * points, -1)

    looked, stamps = lax.optimization_barrier((look(0), stamps))
    stamps = stamps.reshape(owners, BATCHES, cap).swapaxes(0, 1).reshape(BATCHES, -1)
    base_seen = jnp.stack([jnp.take(stamps[b], end_pos[b], mode="clip") for b in range(BATCHES)])
    first, second = exchange(looked), look(1)
    first, second, near_code, gru_in_flat, gru_hid_flat = lax.optimization_barrier(
        (first, second, near_code, gru_in_flat, gru_hid_flat)
    )
    came = [first.reshape(-1, half), exchange(second).reshape(-1, half)]

    results = []
    updated = memory
    fresh_all = None
    for batch in range(BATCHES):
        table = came[batch]
        pick_end = end_slot[batch]
        pick_near = near_slot[batch]
        seen = base_seen[batch]
        if batch > 0:
            ids = jnp.concatenate([end_id[batch], near_id[batch]])
            best = jnp.max(
                jnp.where(all_meta[0][:, None] == ids[None, :], all_meta[1][:, None], -1), axis=0
            )
            written = best >= 0
            index = jnp.where(written, best % total, 0)
            table, results[0] = lax.optimization_barrier((table, results[0]))
            table = jnp.concatenate([table, fresh_all], axis=0)
            block_of = place_by_doubling(index // points, owner_pos, owners)
            newer = owners * slots + block_of * points + index % points
            pick_end = jnp.where(written[:points], newer[:points], pick_end)
            pick_near = jnp.where(written[points:], newer[points:], pick_near)
            since = jnp.take(all_meta[2], index[:points], mode="clip")
            seen = jnp.where(written[:points], since, seen)
        pick_other = pick_end.reshape(events, 2)[:, ::-1].reshape(points)
        picked = jnp.take(
            table, jnp.concatenate([pick_near, pick_end, pick_other]), axis=0, mode="clip"
        )
        full = lax.all_gather(picked, "section", axis=1, tiled=True)
        near_count = neighbors * points
        end_half = picked[near_count : near_count + points].astype(F32)
        end_full = full[near_count : near_count + points]
        other = full[near_count + points :]
        self_code = time_code(time_two[batch] - seen, time_freq, time_phase)
        feat_two = jnp.repeat(edge_feat[batch], 2, axis=0)
        message = jnp.concatenate([end_full, other, self_code, feat_two], axis=1)
        from_msg = jnp.dot(message, gru_in_flat, preferred_element_type=F32)
        from_mem = jnp.dot(end_full, gru_hid_flat, preferred_element_type=F32)

        def block(x, i, side):
            return x[:, i * half : (i + 1) * half] + gru_bias[side, i]

        reset = jax.nn.sigmoid(block(from_msg, 0, 0) + block(from_mem, 0, 1))
        update = jax.nn.sigmoid(block(from_msg, 1, 0) + block(from_mem, 1, 1))
        cand = jnp.tanh(block(from_msg, 2, 0) + reset * block(from_mem, 2, 1))
        fresh = ((1.0 - update) * cand + update * end_half).astype(BF)
        query = jnp.dot(end_full, query_cols, preferred_element_type=F32)
        query, fresh = lax.optimization_barrier((query, fresh))
        wrote = got[:, batch, :cap].reshape(-1) - 1
        order = got[:, batch, slots : slots + cap].reshape(-1)
        if batch + 1 < BATCHES:
            fresh_all = gather_by_doubling(fresh, owners)
            source = place_by_doubling(jnp.arange(owners, dtype=jnp.int32), owner_pos, owners)
            source = source[:, None] * points
            source = source + got[:, batch, slots + cap :]
            values = jnp.take(fresh_all, source.reshape(-1), axis=0, mode="clip")
        else:
            place = jnp.arange(owners * cap, dtype=jnp.int32)[:, None] == end_pos[batch][None, :]
            sent = jnp.dot(place.astype(BF), fresh, preferred_element_type=F32).astype(BF)
            values = exchange(sent.reshape(owners, cap, half)).reshape(-1, half)
        updated = write_rows(updated, wrote, order, values)

        attended = attend(full, near_code[batch], query, wide, twide, neighbors, scale)
        mixed = lax.all_gather(attended, "section", axis=1, tiled=True)
        emb = jnp.dot(mixed, own_cols, precision=lax.Precision.HIGHEST) + end_half
        results.append(emb.astype(BF).reshape(events, 2, half))
    return (updated, jnp.stack(results, axis=0))


def solution(mesh):
    in_specs = (
        P("owner", "section"),
        P("owner"),
        P(None, "owner", None),
        P(None, "owner", None),
        P(None, "owner"),
        P(None, "owner"),
        P(None, "owner", None),
        P(None, "owner", None, None),
        P(None, "owner", None),
        P(None, "owner", None),
        P(),
        P(),
        P(None, None, "section"),
        P(None, None, "section"),
        P(None, None, "section"),
        P(),
        P(),
        P(),
        P(),
        P(),
        P(),
    )
    out_specs = (P("owner", "section"), P(None, "owner", None, "section"))
    return jax.shard_map(
        on_device, mesh=mesh, in_specs=in_specs, out_specs=out_specs, check_vma=False
    )
```

```python
import functools
import math

import jax
import jax.numpy as jnp
from jax import lax
from jax.experimental import pallas as pl
from jax.experimental.pallas import tpu as pltpu
from jax.sharding import PartitionSpec as P

HEADS = 2
BATCHES = 2
BF = jnp.bfloat16
F32 = jnp.float32


def time_code(delta, time_freq, time_phase):
    angle = delta.astype(F32)[..., None] * time_freq + time_phase
    return jnp.cos(angle).astype(BF)


def owner_hits(own, owners):
    return own[..., None] == jnp.arange(owners, dtype=jnp.int32)


def ranks(hits, block):
    batches, total, owners = hits.shape
    parts = total // block
    cut = hits.astype(BF).reshape(batches, parts, block, owners)
    below = jnp.tril(jnp.ones((block, block), BF), -1)
    within = jnp.einsum("ij,bkjo->bkio", below, cut, preferred_element_type=F32)
    sums = jnp.sum(cut.astype(F32), axis=2).astype(BF)
    earlier = jnp.tril(jnp.ones((parts, parts), BF), -1)
    before = jnp.einsum("kl,blo->bko", earlier, sums, preferred_element_type=F32)
    count = within + before[:, :, None]
    picked = jnp.sum(jnp.where(hits.reshape(cut.shape), count, 0.0), axis=3)
    return picked.reshape(batches, total).astype(jnp.int32)


def table_of(hits, rank, size, values):
    place = (rank[..., None] == jnp.arange(size, dtype=jnp.int32)).astype(BF)

    def digit(part):
        lhs = jnp.where(hits, part[..., None].astype(F32), 0.0).astype(BF)
        return jnp.einsum("bno,bns->bos", lhs, place, preferred_element_type=F32)

    return (digit(values // 64) * 64.0 + digit(values % 64)).astype(jnp.int32)


def attend_kernel(scale, group, near, code, query, wide, twide, out, num, den):
    step = pl.program_id(0)
    points, head = query.shape

    @pl.when(step == 0)
    def _():
        num[...] = jnp.zeros_like(num)
        den[...] = jnp.zeros_like(den)

    both = jnp.dot(near[...], wide[...], preferred_element_type=F32) + jnp.dot(
        code[...], twide[...], preferred_element_type=F32
    )
    q = query[...]
    for j in range(group):
        rows = both[j * points : (j + 1) * points]
        score = jnp.sum(rows[:, :head] * q, axis=1, keepdims=True) * scale
        weight = jnp.exp(score)
        den[...] += jnp.broadcast_to(weight, den.shape)
        num[...] += weight * rows[:, head:]

    @pl.when(step == pl.num_programs(0) - 1)
    def _():
        out[...] = num[...] / den[:, :1]


def attend(near, code, query, wide, twide, neighbors, scale):
    points, head = query.shape
    group = next(g for g in (4, 2, 1) if neighbors % g == 0)
    rows = group * points
    return pl.pallas_call(
        functools.partial(attend_kernel, scale, group),
        out_shape=jax.ShapeDtypeStruct((points, head), F32),
        grid=(neighbors // group,),
        in_specs=[
            pl.BlockSpec((rows, near.shape[1]), lambda i: (i, 0)),
            pl.BlockSpec((rows, code.shape[1]), lambda i: (i, 0)),
            pl.BlockSpec(query.shape, lambda i: (0, 0)),
            pl.BlockSpec(wide.shape, lambda i: (0, 0)),
            pl.BlockSpec(twide.shape, lambda i: (0, 0)),
        ],
        out_specs=pl.BlockSpec((points, head), lambda i: (0, 0)),
        scratch_shapes=[pltpu.VMEM((points, head), F32), pltpu.VMEM((points, 128), F32)],
        compiler_params=pltpu.CompilerParams(vmem_limit_bytes=24 * 1024 * 1024),
        cost_estimate=pl.CostEstimate(
            flops=2 * code.shape[0] * (near.shape[1] + code.shape[1]) * wide.shape[1],
            bytes_accessed=2 * code.shape[0] * near.shape[1] + 2 * code.size + 2 * wide.size,
            transcendentals=code.shape[0],
        ),
    )(near, code, query, wide, twide)


def exchange(x):
    return lax.all_to_all(x, "owner", split_axis=0, concat_axis=0, tiled=True)


def gather_by_doubling(x, owners):
    bit = owners // 2
    while bit:
        pairs = [(i, i ^ bit) for i in range(owners)]
        x = jnp.concatenate([x, lax.ppermute(x, "owner", pairs)], axis=0)
        bit //= 2
    return x


def place_by_doubling(owner, this, owners):
    differ, place, bit, unit = owner ^ this, jnp.zeros_like(owner), owners // 2, 1
    while bit:
        place = place + jnp.where((differ & bit) != 0, unit, 0)
        bit, unit = bit // 2, unit * 2
    return place


def write_rows(memory, rows, order, values):
    count = memory.shape[0]
    beaten = jnp.any((rows[:, None] == rows[None, :]) & (order[None, :] > order[:, None]), axis=1)
    place = jnp.where((rows >= 0) & ~beaten, rows, count)
    return memory.at[place].set(values, mode="drop")


def on_device(
    memory,
    last_seen,
    ends_owner,
    ends_row,
    event_order,
    event_time,
    edge_feat,
    nb_owner,
    nb_row,
    nb_time,
    time_freq,
    time_phase,
    gru_in,
    gru_hid,
    gru_bias,
    query_w,
    key_w,
    value_w,
    time_key,
    time_value,
    out_w,
):
    owners = lax.axis_size("owner")
    sections = lax.axis_size("section")
    count, half = memory.shape
    width = half * sections
    events = ends_owner.shape[1]
    points = 2 * events
    neighbors = nb_row.shape[2] // 2
    head_dim = width // HEADS
    cap = max(4, 4 * events // owners)
    capn = max(8, 3 * neighbors * events // owners)
    slots = cap + capn
    total = owners * points
    scale = 1.0 / math.sqrt(head_dim)
    section_pos = lax.axis_index("section")
    owner_pos = lax.axis_index("owner")

    def by_neighbor(x):
        return x.reshape(BATCHES, points, neighbors).swapaxes(1, 2)

    end_own = ends_owner.reshape(BATCHES, points)
    end_row = ends_row.reshape(BATCHES, points)
    near_own = by_neighbor(nb_owner[..., 0]).reshape(BATCHES, -1)
    near_row = by_neighbor(nb_row).reshape(BATCHES, -1)
    order_two = jnp.repeat(event_order, 2, axis=1)
    time_two = jnp.repeat(event_time, 2, axis=1)
    end_hits = owner_hits(end_own, owners)
    near_hits = owner_hits(near_own, owners)
    end_rank = ranks(end_hits, points)
    near_rank = ranks(near_hits, points)
    local = jnp.broadcast_to(jnp.arange(points, dtype=jnp.int32), (BATCHES, points))
    asked = jnp.concatenate(
        [
            table_of(end_hits, end_rank, cap, end_row + 1),
            table_of(near_hits, near_rank, capn, near_row + 1),
            table_of(end_hits, end_rank, cap, order_two),
            table_of(end_hits, end_rank, cap, local),
        ],
        axis=2,
    )
    end_id = end_own * count + end_row
    near_id = near_own * count + near_row
    mine = owner_pos * points + jnp.arange(points, dtype=jnp.int32)
    meta = jnp.concatenate([end_id[0], order_two[0] * total + mine, time_two[0]])
    per_batch = slots + 2 * cap
    asked = jnp.concatenate(
        [
            asked.swapaxes(0, 1).reshape(owners, BATCHES * per_batch),
            jnp.broadcast_to(meta, (owners, 3 * points)),
        ],
        axis=1,
    )
    answer = exchange(asked)
    got = answer[:, : BATCHES * per_batch].reshape(owners, BATCHES, per_batch)
    all_meta = answer[:, BATCHES * per_batch :].reshape(owners, 3, points)
    all_meta = [all_meta[:, i].reshape(total) for i in range(3)]
    end_pos = end_own * cap + end_rank
    end_slot = end_own * slots + end_rank
    near_slot = near_own * slots + cap + near_rank

    asked_ends = jnp.maximum(got[:, :, :cap] - 1, 0).reshape(-1)
    stamps = jnp.take(last_seen, asked_ends, mode="clip").reshape(owners, BATCHES * cap)
    stamps = exchange(stamps)

    def look(batch):
        rows = jnp.maximum(got[:, batch, :slots] - 1, 0).reshape(-1)
        return jnp.take(memory, rows, axis=0, mode="clip").reshape(owners, slots, half)

    start = section_pos * head_dim

    def columns(w, at, size):
        return lax.dynamic_slice_in_dim(w, at, size, 1)

    wide = jnp.concatenate([columns(key_w, start, head_dim), columns(value_w, start, head_dim)], axis=1)
    twide = jnp.concatenate(
        [columns(time_key, start, head_dim), columns(time_value, start, head_dim)], axis=1
    )
    query_cols = columns(query_w, start, head_dim)
    own_cols = columns(out_w, section_pos * half, half).astype(F32)
    gru_in_flat = gru_in.reshape(gru_in.shape[0], 3 * half)
    gru_hid_flat = gru_hid.reshape(width, 3 * half)
    near_code = time_code(time_two[:, None] - by_neighbor(nb_time), time_freq, time_phase)
    near_code = near_code.reshape(BATCHES, neighbors * points, -1)

    looked, stamps = lax.optimization_barrier((look(0), stamps))
    stamps = stamps.reshape(owners, BATCHES, cap).swapaxes(0, 1).reshape(BATCHES, -1)
    base_seen = jnp.stack([jnp.take(stamps[b], end_pos[b], mode="clip") for b in range(BATCHES)])
    first, second = exchange(looked), look(1)
    first, second, near_code, gru_in_flat, gru_hid_flat = lax.optimization_barrier(
        (first, second, near_code, gru_in_flat, gru_hid_flat)
    )
    came = [first.reshape(-1, half)]

    results = []
    updated = memory
    fresh_all = None
    for batch in range(BATCHES):
        table = came[batch]
        pick_end = end_slot[batch]
        pick_near = near_slot[batch]
        seen = base_seen[batch]
        if batch > 0:
            ids = jnp.concatenate([end_id[batch], near_id[batch]])
            best = jnp.max(
                jnp.where(all_meta[0][:, None] == ids[None, :], all_meta[1][:, None], -1), axis=0
            )
            written = best >= 0
            index = jnp.where(written, best % total, 0)
            table, results[0] = lax.optimization_barrier((table, results[0]))
            table = jnp.concatenate([table, fresh_all], axis=0)
            block_of = place_by_doubling(index // points, owner_pos, owners)
            newer = owners * slots + block_of * points + index % points
            pick_end = jnp.where(written[:points], newer[:points], pick_end)
            pick_near = jnp.where(written[points:], newer[points:], pick_near)
            since = jnp.take(all_meta[2], index[:points], mode="clip")
            seen = jnp.where(written[:points], since, seen)
        pick_other = pick_end.reshape(events, 2)[:, ::-1].reshape(points)
        picked = jnp.take(
            table, jnp.concatenate([pick_near, pick_end, pick_other]), axis=0, mode="clip"
        )
        full = lax.all_gather(picked, "section", axis=1, tiled=True)
        near_count = neighbors * points
        end_half = picked[near_count : near_count + points].astype(F32)
        end_full = full[near_count : near_count + points]
        other = full[near_count + points :]
        self_code = time_code(time_two[batch] - seen, time_freq, time_phase)
        feat_two = jnp.repeat(edge_feat[batch], 2, axis=0)
        message = jnp.concatenate([end_full, other, self_code, feat_two], axis=1)
        from_msg = jnp.dot(message, gru_in_flat, preferred_element_type=F32)
        from_mem = jnp.dot(end_full, gru_hid_flat, preferred_element_type=F32)

        def block(x, i, side):
            return x[:, i * half : (i + 1) * half] + gru_bias[side, i]

        reset = jax.nn.sigmoid(block(from_msg, 0, 0) + block(from_mem, 0, 1))
        update = jax.nn.sigmoid(block(from_msg, 1, 0) + block(from_mem, 1, 1))
        cand = jnp.tanh(block(from_msg, 2, 0) + reset * block(from_mem, 2, 1))
        fresh = ((1.0 - update) * cand + update * end_half).astype(BF)
        query = jnp.dot(end_full, query_cols, preferred_element_type=F32)
        query, fresh = lax.optimization_barrier((query, fresh))
        wrote = got[:, batch, :cap].reshape(-1) - 1
        order = got[:, batch, slots : slots + cap].reshape(-1)
        if batch + 1 < BATCHES:
            fresh_all = gather_by_doubling(fresh, owners)
            second, fresh_all = lax.optimization_barrier((second, fresh_all))
            came.append(exchange(second).reshape(-1, half))
            source = place_by_doubling(jnp.arange(owners, dtype=jnp.int32), owner_pos, owners)
            source = source[:, None] * points
            source = source + got[:, batch, slots + cap :]
            values = jnp.take(fresh_all, source.reshape(-1), axis=0, mode="clip")
        else:
            place = jnp.arange(owners * cap, dtype=jnp.int32)[:, None] == end_pos[batch][None, :]
            sent = jnp.dot(place.astype(BF), fresh, preferred_element_type=F32).astype(BF)
            values = exchange(sent.reshape(owners, cap, half)).reshape(-1, half)
        updated = write_rows(updated, wrote, order, values)

        attended = attend(full, near_code[batch], query, wide, twide, neighbors, scale)
        mixed = lax.all_gather(attended, "section", axis=1, tiled=True)
        emb = jnp.dot(mixed, own_cols, precision=lax.Precision.HIGHEST) + end_half
        results.append(emb.astype(BF).reshape(events, 2, half))
    return (updated, jnp.stack(results, axis=0))


def solution(mesh):
    in_specs = (
        P("owner", "section"),
        P("owner"),
        P(None, "owner", None),
        P(None, "owner", None),
        P(None, "owner"),
        P(None, "owner"),
        P(None, "owner", None),
        P(None, "owner", None, None),
        P(None, "owner", None),
        P(None, "owner", None),
        P(),
        P(),
        P(None, None, "section"),
        P(None, None, "section"),
        P(None, None, "section"),
        P(),
        P(),
        P(),
        P(),
        P(),
        P(),
    )
    out_specs = (P("owner", "section"), P(None, "owner", None, "section"))
    return jax.shard_map(
        on_device, mesh=mesh, in_specs=in_specs, out_specs=out_specs, check_vma=False
    )
```
